256 devices in a mesh: leaf: 256 (over x, y, z, core).
Axes of the slice: x: 4, y: 4, z: 8, core: 2. Of those that a mesh axis runs over, the one named last changes fastest.
Arguments:
- right_sides: float32 [64, 262144], P(None, 'leaf'), may hold values from -6 to 6
- leaf_inverse: float32 [262144, 1024], P('leaf'), may hold values from -1.5 to 1.5
- coupling_first: float32 [262144, 256], P('leaf'), may hold values from -0.046875 to 0.046875
- coupling_second: float32 [262144, 256], P('leaf'), may hold values from -0.03125 to 0.03125
- coupling_third: float32 [262144, 256], P('leaf'), may hold values from -0.0234375 to 0.0234375
- coupling_fourth: float32 [262144, 256], P('leaf'), may hold values from -0.015625 to 0.015625
- solved_first: float32 [262144, 256], P('leaf'), may hold values from -0.375 to 0.375
- solved_second: float32 [262144, 256], P('leaf'), may hold values from -0.375 to 0.375
- solved_third: float32 [262144, 256], P('leaf'), may hold values from -0.375 to 0.375
- solved_fourth: float32 [262144, 256], P('leaf'), may hold values from -0.375 to 0.375
- first_level_inverse: float32 [4096, 512], P('leaf'), may hold values from -1.5 to 1.5
- second_level_inverse: float32 [2048, 512], P('leaf'), may hold values from -1.5 to 1.5
- third_level_inverse: float32 [1024, 512], P('leaf'), may hold values from -1.5 to 1.5
- root_level_inverse: float32 [512, 512], P('leaf'), may hold values from -1.5 to 1.5
Outputs:
- solution: float32 [64, 262144], P(None, 'leaf')
The draws below stay inside these ranges and needn't reach their ends.
All inputs are finite; a program needn't handle non-finite values.
Results may differ from the reference program's by a relative error of at most 0.00028.
Values sent between devices are 32-bit elements; how exact they have to be, the bound alone decides.
No kernel may reach another device: no remote copies, remote signals or barrier semaphores. Data moves between devices by JAX's collectives and lax.ppermute only.
A program may use at most 64 MiB of HBM per device.

```python
import math
import jax
import jax.numpy as jnp
from jax import lax

LEAF = 1024
RANK = 256
NRHS = 64
TREE_HEIGHT = 8
POINTS = 262144
N_LEAF = 256


def dominant(key, row_count, width):
    row_ids = lax.broadcasted_iota(jnp.int32, (row_count, width), 0) % width
    col_ids = lax.broadcasted_iota(jnp.int32, (row_count, width), 1)
    noise = jax.random.truncated_normal(key, -4.0, 4.0, (row_count, width), jnp.float32) * (0.5 / math.sqrt(width))
    return jnp.where(row_ids == col_ids, 1.0, 0.0).astype(jnp.float32) + noise


def draw_leaf_inverse(key, part):
    key = jax.random.fold_in(key, 11)
    return dominant(key, POINTS, LEAF)


def draw_first_level_inverse(key, part):
    key = jax.random.fold_in(key, 21)
    return dominant(key, 16 * RANK, 2 * RANK)


def draw_second_level_inverse(key, part):
    key = jax.random.fold_in(key, 31)
    return dominant(key, 8 * RANK, 2 * RANK)


def draw_third_level_inverse(key, part):
    key = jax.random.fold_in(key, 41)
    return dominant(key, 4 * RANK, 2 * RANK)


def draw_root_level_inverse(key, part):
    key = jax.random.fold_in(key, 51)
    return dominant(key, 2 * RANK, 2 * RANK)


def steps_of(own_key, extent, pieces, low, top_value):
    def one(position, shards_of):
        draws = jax.random.uniform(jax.random.fold_in(jax.random.fold_in(own_key, 6), position), (shards_of,), jnp.float32, low / len(pieces), top_value / len(pieces))
        return jnp.repeat(jnp.exp(draws), extent[position] // shards_of).reshape((-1,) + (1,) * (len(extent) - position - 1))

    loudness = one(*pieces[0])
    for cut in pieces[1:]:
        loudness = loudness * one(*cut)
    return loudness


def centred(stream_key, dims, scale, limit, cuts=(), held_as=jnp.bfloat16):
    level = steps_of(stream_key, dims, cuts, -0.22, 0.18) if cuts else 1.0
    array = jax.random.normal(stream_key, dims, jnp.float32) * scale * level
    return jnp.minimum(jnp.maximum(array, -limit), limit).astype(held_as)


def setup_inputs(seed: int = 0) -> dict:
    streams_of = jax.random.split(jax.random.key(seed), 15)
    right_sides = centred(streams_of[0], (NRHS, POINTS), 1.0, 6.0, ((1, 256),), jnp.float32)
    leaf_inverse = draw_leaf_inverse(jax.random.fold_in(streams_of[14], 71), 0)
    coupling_first = centred(streams_of[2], (POINTS, RANK), (LEAF * N_LEAF // 16) ** -0.5, 0.046875, ((0, 256),), jnp.float32)
    coupling_second = centred(streams_of[3], (POINTS, RANK), (LEAF * N_LEAF // 8) ** -0.5, 0.03125, ((0, 256),), jnp.float32)
    coupling_third = centred(streams_of[4], (POINTS, RANK), (LEAF * N_LEAF // 4) ** -0.5, 0.0234375, ((0, 256),), jnp.float32)
    coupling_fourth = centred(streams_of[5], (POINTS, RANK), (LEAF * N_LEAF // 2) ** -0.5, 0.015625, ((0, 256),), jnp.float32)
    solved_first = centred(streams_of[6], (POINTS, RANK), RANK ** -0.5, 0.375, ((0, 256),), jnp.float32)
    solved_second = centred(streams_of[7], (POINTS, RANK), RANK ** -0.5, 0.375, ((0, 256),), jnp.float32)
    solved_third = centred(streams_of[8], (POINTS, RANK), RANK ** -0.5, 0.375, ((0, 256),), jnp.float32)
    solved_fourth = centred(streams_of[9], (POINTS, RANK), RANK ** -0.5, 0.375, ((0, 256),), jnp.float32)
    first_level_inverse = draw_first_level_inverse(jax.random.fold_in(streams_of[14], 71), 0)
    second_level_inverse = draw_second_level_inverse(jax.random.fold_in(streams_of[14], 71), 0)
    third_level_inverse = draw_third_level_inverse(jax.random.fold_in(streams_of[14], 71), 0)
    root_level_inverse = draw_root_level_inverse(jax.random.fold_in(streams_of[14], 71), 0)
    return {"right_sides": right_sides, "leaf_inverse": leaf_inverse, "coupling_first": coupling_first, "coupling_second": coupling_second, "coupling_third": coupling_third, "coupling_fourth": coupling_fourth, "solved_first": solved_first, "solved_second": solved_second, "solved_third": solved_third, "solved_fourth": solved_fourth, "first_level_inverse": first_level_inverse, "second_level_inverse": second_level_inverse, "third_level_inverse": third_level_inverse, "root_level_inverse": root_level_inverse}


def apply_tree_level(running_solution, coupling, solved, capacity, level_bit):
    halves = N_LEAF >> level_bit
    span = LEAF << level_bit
    groups = halves // 2
    shaped = running_solution.reshape(NRHS, halves, span)
    sums = jnp.einsum("nhp,hpr->hnr", shaped, coupling.reshape(halves, span, RANK), precision=lax.Precision.HIGHEST)
    pair_sums = sums.reshape(groups, 2, NRHS, RANK)
    stacked = jnp.concatenate([pair_sums[:, 1], pair_sums[:, 0]], axis=2)
    weights = jnp.einsum("gnk,gik->gni", stacked, capacity.reshape(groups, 2 * RANK, 2 * RANK), precision=lax.Precision.HIGHEST)
    half_weights = weights.reshape(groups, NRHS, 2, RANK).transpose(0, 2, 1, 3).reshape(halves, NRHS, RANK)
    correction = jnp.einsum("hnr,hpr->nhp", half_weights, solved.reshape(halves, span, RANK), precision=lax.Precision.HIGHEST)
    return (shaped - correction).reshape(NRHS, POINTS)


def reference(right_sides, leaf_inverse, coupling_first, coupling_second, coupling_third, coupling_fourth, solved_first, solved_second, solved_third, solved_fourth, first_level_inverse, second_level_inverse, third_level_inverse, root_level_inverse):
    blocks = right_sides.reshape(NRHS, N_LEAF, LEAF)
    running_solution = jnp.einsum("nlk,lik->nli", blocks, leaf_inverse.reshape(N_LEAF, LEAF, LEAF), precision=lax.Precision.HIGHEST).reshape(NRHS, POINTS)
    coupling_factors = [coupling_first, coupling_second, coupling_third, coupling_fourth]
    solved_blocks = [solved_first, solved_second, solved_third, solved_fourth]
    capacitance_inverses = [first_level_inverse, second_level_inverse, third_level_inverse, root_level_inverse]
    for level_number in range(4):
        running_solution = apply_tree_level(running_solution, coupling_factors[level_number], solved_blocks[level_number], capacitance_inverses[level_number], TREE_HEIGHT - 4 + level_number)
    return running_solution
```

```python
import jax
import jax.numpy as jnp
from jax import lax
from jax.sharding import PartitionSpec as P

CORE, Z_LOW, Z_MID, Z_FLIP = 1, 2, 4, 14
Y_LOW, Y_FLIP, X_LOW, X_FLIP = 16, 48, 64, 192


def swapped(value, mask):
    pairs = [(source, source ^ mask) for source in range(lax.axis_size("leaf"))]
    return lax.ppermute(value, "leaf", pairs)


def product(left, right, dims, precision=lax.Precision.HIGH):
    return lax.dot_general(
        left,
        right,
        ((dims[:1], dims[1:]), ((), ())),
        precision=precision,
        preferred_element_type=jnp.float32,
    )


def product_nn(left, right):
    return product(left, right, (1, 0))


def product_nt(left, right):
    return product(left, right, (1, 1))


def product_tn(left, right):
    return product(left, right, (0, 0))


def summed(value, masks):
    for mask in masks:
        value = value + swapped(value, mask)
    return value


def split_sum(value, bit, mask):
    half = value.shape[0] // 2
    low, high = value[:half], value[half:]
    kept = jnp.where(bit, high, low)
    sent = jnp.where(bit, low, high)
    return kept + swapped(sent, mask)


def ordered(own, other, bit, axis=0):
    return jnp.where(
        bit,
        jnp.concatenate([other, own], axis=axis),
        jnp.concatenate([own, other], axis=axis),
    )


def joined(value, bit, mask, axis=0):
    return ordered(value, swapped(value, mask), bit, axis)


def gather_first(capacity, bits):
    rows, width = capacity.shape
    held = joined(capacity, bits[3], Z_FLIP)
    held = joined(held, bits[2] != bits[3], Z_MID)
    held = joined(held, bits[1] != bits[3], Z_LOW)
    held = joined(held, bits[0], CORE)
    held = held.reshape(2, 2, 2, 2, rows, width)
    low = held[:, :, :, 0].transpose(2, 1, 0, 3, 4)
    high = held[:, ::-1, ::-1, 1].transpose(2, 1, 0, 3, 4)
    return jnp.stack([low, high]).reshape(16 * rows, width)


def gather_rest(second, third, fourth, bits):
    width = second.shape[1]
    a, b, c = second.shape[0], third.shape[0], fourth.shape[0]
    other = swapped(jnp.concatenate([second, third, fourth]), Y_LOW)
    second = ordered(second, other[:a], bits[4])
    third = ordered(third, other[a : a + b], bits[4])
    fourth = ordered(fourth, other[a + b :], bits[4])
    other = swapped(jnp.concatenate([third, fourth]), Y_FLIP)
    third = ordered(third, other[: 2 * b], bits[5])
    fourth = ordered(fourth, other[2 * b :], bits[5])
    fourth = joined(fourth, bits[6], X_LOW)
    rows = second.shape[0]
    count = lax.axis_size("leaf")
    groups = [list(range(first, first + 16)) for first in range(0, count, 16)]
    whole = lax.all_gather(
        jnp.concatenate([second, third, fourth]), "leaf", axis_index_groups=groups
    )
    out = []
    for number, block in enumerate((a, b, c)):
        part = whole[:, number * rows : (number + 1) * rows]
        part = part.reshape(16, rows // block, block, width).transpose(1, 0, 2, 3)
        out.append(part.reshape(16 * rows, width))
    return out


def cross_terms(solved_second, solved_third, coupling_third, coupling_fourth, bits):
    rank = coupling_third.shape[1]
    second = product_tn(
        solved_second, jnp.concatenate([coupling_third, coupling_fourth], axis=1)
    )
    third = product_tn(solved_third, coupling_fourth)
    both = jnp.concatenate([second, third], axis=1)
    both = split_sum(both, bits[0], CORE)
    low, mid = bits[1] != bits[3], bits[2] != bits[3]
    both = split_sum(both, low, Z_LOW)
    both = split_sum(both, mid, Z_MID)
    both = summed(both, (Z_FLIP, Y_LOW))
    both = jnp.concatenate(
        [both[:, : 2 * rank], summed(both[:, 2 * rank :], (Y_FLIP,))], axis=1
    )
    both = joined(both, mid, Z_MID)
    both = joined(both, low, Z_LOW)
    both = joined(both, bits[0], CORE)
    return both[:, : 2 * rank], both[:, 2 * rank :]


def weights_of(own, mask, bit, capacity):
    return product_nt(ordered(own, swapped(own, mask), ~bit, axis=1), capacity)


def per_device(
    right_sides,
    leaf_inverse,
    coupling_first,
    coupling_second,
    coupling_third,
    coupling_fourth,
    solved_first,
    solved_second,
    solved_third,
    solved_fourth,
    first_level_inverse,
    second_level_inverse,
    third_level_inverse,
    root_level_inverse,
):
    rank = coupling_first.shape[1]
    device_id = lax.axis_index("leaf")
    bits = [(device_id >> place) & 1 == 1 for place in range(8)]
    capacity_first = gather_first(first_level_inverse, bits)
    capacity_second, capacity_third, capacity_fourth = gather_rest(
        second_level_inverse, third_level_inverse, root_level_inverse, bits
    )
    cross_second, cross_third = cross_terms(
        solved_second, solved_third, coupling_third, coupling_fourth, bits
    )

    current = product_nt(right_sides, leaf_inverse)

    sums = split_sum(product_nn(current, coupling_first), bits[0], CORE)
    sums = summed(sums, (Z_LOW, Z_MID, Z_FLIP))
    weights = weights_of(sums, Y_LOW, bits[4], capacity_first)
    weights = joined(weights, bits[0], CORE)
    current = current - product_nt(weights, solved_first)

    coupling = jnp.concatenate([coupling_second, coupling_third, coupling_fourth], axis=1)
    sums = split_sum(product_nn(current, coupling), bits[0], CORE)
    sums = summed(sums, (Z_LOW, Z_MID, Z_FLIP, Y_LOW))
    second = weights_of(sums[:, :rank], Y_FLIP, bits[5], capacity_second)
    sums = sums[:, rank:] - product_nn(second, cross_second)
    sums = summed(sums, (Y_FLIP,))
    third = weights_of(sums[:, :rank], X_LOW, bits[6], capacity_third)
    sums = sums[:, rank:] - product_nn(third, cross_third)
    sums = summed(sums, (X_LOW,))
    fourth = weights_of(sums, X_FLIP, bits[7], capacity_fourth)
    weights = joined(jnp.concatenate([second, third, fourth], axis=1), bits[0], CORE)
    solved = jnp.concatenate([solved_second, solved_third, solved_fourth], axis=1)
    return current - product_nt(weights, solved)


def solution(mesh):
    in_specs = (P(None, "leaf"),) + (P("leaf", None),) * 13
    return jax.shard_map(
        per_device,
        mesh=mesh,
        in_specs=in_specs,
        out_specs=P(None, "leaf"),
        check_vma=False,
    )
```

```python
import jax
import jax.numpy as jnp
import numpy as np
from jax import lax
from jax.experimental.layout import Layout, with_layout_constraint
from jax.sharding import PartitionSpec as P

CORE, Y_A, Y_B, X_A, X_B = ([i ^ m for i in range(256)] for m in (1, 16, 48, 64, 192))


def ring_pairs(partner):
    return [i - i % 16 + 2 * partner[i // 2 % 8] + i % 2 for i in range(256)]


Z_A = ring_pairs([1, 0, 3, 2, 5, 4, 7, 6])
Z_B = ring_pairs([7, 2, 1, 4, 3, 6, 5, 0])
Z_C = ring_pairs([3, 6, 5, 0, 7, 2, 1, 4])
SIDE_A, SIDE_B, SIDE_C = 0b01100110, 0b10110100, 0b11101000
RING_ORDER = [0, 3, 4, 7, 1, 6, 2, 5]


def tree_order(groups, rows):
    size = 16 * groups * rows
    source = [
        ((group * 8 + z) * 2 + core) * rows + row
        for core in range(2)
        for group in range(groups)
        for z in RING_ORDER
        for row in range(rows)
    ]
    matrix = np.zeros((size, size), np.float32)
    matrix[np.arange(size), source] = 1
    return matrix


def by_rows(value):
    return with_layout_constraint(value, Layout(major_to_minor=(0, 1)))


def together(*values):
    return lax.optimization_barrier(values)


def swapped(value, partner):
    return lax.ppermute(value, "leaf", list(enumerate(partner)))


def sent(partner, *parts):
    got = swapped(jnp.concatenate(parts), partner)
    ends = [0]
    for part in parts:
        ends.append(ends[-1] + part.shape[0])
    return [got[first:last] for first, last in zip(ends, ends[1:])]


def product(left, right, dims, precision=lax.Precision.HIGH):
    return lax.dot_general(
        left,
        right,
        ((dims[:1], dims[1:]), ((), ())),
        precision=precision,
        preferred_element_type=jnp.float32,
    )


def product_nn(left, right):
    return product(left, right, (1, 0))


def product_nt(left, right):
    return product(left, right, (1, 1))


def product_tn(left, right):
    return product(left, right, (0, 0))


def halves(value, side, blocks=1):
    value = value.reshape(blocks, 2, -1, value.shape[1])
    kept = jnp.where(side, value[:, 1], value[:, 0])
    other = jnp.where(side, value[:, 0], value[:, 1])
    return kept.reshape(-1, value.shape[3]), other.reshape(-1, value.shape[3])


def ordered(own, other, side, blocks=1):
    width = own.shape[1]
    own, other = own.reshape(blocks, -1, width), other.reshape(blocks, -1, width)
    both = jnp.where(
        side,
        jnp.concatenate([other, own], axis=1),
        jnp.concatenate([own, other], axis=1),
    )
    return both.reshape(-1, width)


def two_halves(capacity):
    rank = capacity.shape[1] // 2
    return jnp.concatenate([capacity[:, :rank], capacity[:, rank:]])


def solved_weights(own, other, side, capacity, order):
    upper, lower = jnp.where(side, own, other), jnp.where(side, other, own)
    rank = capacity.shape[1]
    weights = product_nt(upper, capacity[:rank]) + product_nt(lower, capacity[rank:])
    return product_nn(weights, order)


def corrected(current, weights, solved, core):
    weights = ordered(weights, swapped(weights, CORE), core)
    return current - product_nt(weights, solved)


def per_device(
    right_sides,
    leaf_inverse,
    coupling_first,
    coupling_second,
    coupling_third,
    coupling_fourth,
    solved_first,
    solved_second,
    solved_third,
    solved_fourth,
    first_level_inverse,
    second_level_inverse,
    third_level_inverse,
    root_level_inverse,
):
    rank = coupling_first.shape[1]
    device_id = lax.axis_index("leaf")
    core, y_low, y_high, x_low, x_high = (
        (device_id >> place) & 1 == 1 for place in (0, 4, 5, 6, 7)
    )
    z = (device_id >> 1) & 7
    side_a, side_b, side_c = ((side >> z) & 1 == 1 for side in (SIDE_A, SIDE_B, SIDE_C))
    y_side = y_low != y_high
    sizes = [
        level.shape[0]
        for level in (second_level_inverse, third_level_inverse, root_level_inverse)
    ]
    orders = [
        jnp.asarray(tree_order(2**level, first_level_inverse.shape[0] >> level))
        for level in range(4)
    ]

    current = product_nt(right_sides, leaf_inverse)
    kept, away = halves(product_nn(current, coupling_first), core)

    away, *inputs = together(
        away,
        first_level_inverse,
        second_level_inverse,
        third_level_inverse,
        root_level_inverse,
        solved_second,
        solved_third,
    )
    sums = kept + swapped(away, CORE)
    near = two_halves(inputs[0])
    far = jnp.zeros((first_level_inverse.shape[0] - sum(sizes), 2 * rank), jnp.float32)
    far = two_halves(jnp.concatenate([*inputs[1:4], far]))
    cross = by_rows(
        jnp.concatenate(
            [
                product_tn(inputs[4], coupling_third),
                product_tn(inputs[4], coupling_fourth),
                product_tn(inputs[5], coupling_fourth),
            ]
        )
    )

    sums, near, far = together(sums, near, far)
    other, near_other, far_other = sent(Z_C, sums, near, far)
    cross, cross_away = halves(cross, core, 3)
    cross = cross + swapped(cross_away, CORE)
    sums = sums + other
    near, far = ordered(near, near_other, side_c, 2), ordered(far, far_other, side_c, 2)

    cross, cross_away = halves(cross, y_side, 3)
    sums, near, far, cross_away = together(sums, near, far, cross_away)
    other, near_other, far_other = sent(Z_B, sums, near, far)
    cross = cross + swapped(cross_away, Y_A)
    sums = sums + other
    near, far = ordered(near, near_other, side_b, 2), ordered(far, far_other, side_b, 2)

    sums, near, cross = together(sums, near, cross)
    other, near_other = sent(Z_A, sums, near)
    last = cross.shape[0] // 3 * 2
    cross = jnp.concatenate([cross[:last], cross[last:] + swapped(cross[last:], Y_B)])
    sums, near = sums + other, ordered(near, near_other, side_a, 2)

    cross, cross_away = halves(cross, side_a, 3)
    sums, near, cross_away = together(sums, near, cross_away)
    other = swapped(sums, Y_A)
    near = ordered(near, swapped(near, CORE), core, 2)
    cross = cross + swapped(cross_away, Z_A)
    first = solved_weights(sums, other, y_low, near, orders[0])

    cross, cross_away = halves(cross, side_b, 3)
    first, cross_away, far = together(first, cross_away, far)
    cross_other = swapped(cross_away, Z_B)
    far_other = swapped(far, Z_A)
    current = corrected(current, first, solved_first, core)

    sums = [
        product_nn(current, coupling)
        for coupling in (coupling_second, coupling_third, coupling_fourth)
    ]
    kept, away = halves(jnp.concatenate(sums), core, 3)
    cross = cross + cross_other
    far = ordered(far, far_other, side_a, 2).reshape(16, -1, rank)
    ends = [0, sizes[0], sizes[0] + sizes[1], sum(sizes)]
    far = [far[:, a:b].reshape(-1, rank) for a, b in zip(ends, ends[1:])]

    away, cross, *far = together(away, cross, *far)
    sums = kept + swapped(away, CORE)
    share = sums.shape[0] // 3
    cross_other = swapped(cross, Z_C)
    far_other = sent(Y_A, *far)

    sums, = together(sums)
    sums = sums + swapped(sums, Z_A)

    cross = cross + cross_other
    far = [ordered(own, got, y_low, 2) for own, got in zip(far, far_other)]
    sums, cross, *far = together(sums, cross, *far)
    other, cross_other = sent(Z_B, sums, cross)
    far_other = sent(Y_B, *far[1:])
    sums, cross = sums + other, ordered(cross, cross_other, side_b, 3)

    far[1:] = [ordered(own, got, y_high, 2) for own, got in zip(far[1:], far_other)]
    sums, cross, *far = together(sums, cross, *far)
    other = swapped(sums, Z_C)
    cross = ordered(cross, swapped(cross, Z_A), side_a, 3)
    far[0] = ordered(far[0], swapped(far[0], CORE), core, 2)
    sums = sums + other

    sums, cross, *far = together(sums, cross, *far)
    other = swapped(sums, Y_A)
    cross = ordered(cross, swapped(cross, Y_A), y_side, 3)
    far_other = swapped(far[2], X_A)
    far[1] = ordered(far[1], swapped(far[1], CORE), core, 2)
    sums = sums + other

    sums, cross, *far = together(sums, cross, *far)
    own = sums[:share]
    other = swapped(own, Y_B)
    cross = ordered(cross, swapped(cross, CORE), core, 3)
    second = solved_weights(own, other, y_high, far[0], orders[1])
    sums = sums[share:] - jnp.concatenate(
        [product_nn(second, cross[:rank]), product_nn(second, cross[rank : 2 * rank])]
    )

    sums, second, cross, *far = together(sums, second, cross, far[1], far[2], far_other)
    sums = sums + swapped(sums, Y_B)
    capacity = ordered(far[1], far[2], x_low, 2)
    capacity = ordered(capacity, swapped(capacity, CORE), core, 2)
    current = corrected(current, second, solved_second, core)

    sums, current, capacity = together(sums, current, capacity)
    own = sums[:share]
    third = solved_weights(own, swapped(own, X_A), x_low, far[0], orders[2])
    sums = sums[share:] - product_nn(third, cross[2 * rank :])

    sums, third = together(sums, third)
    sums = sums + swapped(sums, X_A)
    current = corrected(current, third, solved_third, core)

    sums, current = together(sums, current)
    fourth = solved_weights(sums, swapped(sums, X_B), x_high, capacity, orders[3])
    return corrected(current, fourth, solved_fourth, core)


def solution(mesh):
    in_specs = (P(None, "leaf"),) + (P("leaf", None),) * 13
    return jax.shard_map(
        per_device,
        mesh=mesh,
        in_specs=in_specs,
        out_specs=P(None, "leaf"),
        check_vma=False,
    )
```

```python
import jax
import jax.numpy as jnp
import numpy as np
from jax import lax
from jax.experimental.layout import Layout, with_layout_constraint
from jax.sharding import PartitionSpec as P

CORE, Y_A, Y_B, X_A, X_B = ([i ^ m for i in range(256)] for m in (1, 16, 48, 64, 192))


def ring_pairs(partner):
    return [i - i % 16 + 2 * partner[i // 2 % 8] + i % 2 for i in range(256)]


Z_A = ring_pairs([1, 0, 3, 2, 5, 4, 7, 6])
Z_B = ring_pairs([7, 2, 1, 4, 3, 6, 5, 0])
Z_C = ring_pairs([3, 6, 5, 0, 7, 2, 1, 4])
SIDE_A, SIDE_B, SIDE_C = 0b01100110, 0b10110100, 0b11101000
RING_ORDER = [0, 3, 4, 7, 1, 6, 2, 5]


def tree_order(groups, rows):
    size = 16 * groups * rows
    source = [
        ((group * 8 + z) * 2 + core) * rows + row
        for core in range(2)
        for group in range(groups)
        for z in RING_ORDER
        for row in range(rows)
    ]
    matrix = np.zeros((size, size), np.float32)
    matrix[np.arange(size), source] = 1
    return matrix


def by_rows(value):
    return with_layout_constraint(value, Layout(major_to_minor=(0, 1)))


def after(value, token):
    return lax.optimization_barrier((value, token))[0]


def swapped(value, partner):
    return lax.ppermute(value, "leaf", list(enumerate(partner)))


def sent(partner, *parts):
    got = swapped(jnp.concatenate(parts), partner)
    ends = [0]
    for part in parts:
        ends.append(ends[-1] + part.shape[0])
    return [got[first:last] for first, last in zip(ends, ends[1:])]


def product(left, right, dims, precision=lax.Precision.HIGH):
    return lax.dot_general(
        left,
        right,
        ((dims[:1], dims[1:]), ((), ())),
        precision=precision,
        preferred_element_type=jnp.float32,
    )


def product_nn(left, right):
    return product(left, right, (1, 0))


def product_nt(left, right):
    return product(left, right, (1, 1))


def product_tn(left, right):
    return product(left, right, (0, 0))


def halves(value, side, blocks=1):
    value = value.reshape(blocks, 2, -1, value.shape[1])
    kept = jnp.where(side, value[:, 1], value[:, 0])
    other = jnp.where(side, value[:, 0], value[:, 1])
    return kept.reshape(-1, value.shape[3]), other.reshape(-1, value.shape[3])


def ordered(own, other, side, blocks=1):
    width = own.shape[1]
    own, other = own.reshape(blocks, -1, width), other.reshape(blocks, -1, width)
    both = jnp.where(
        side,
        jnp.concatenate([other, own], axis=1),
        jnp.concatenate([own, other], axis=1),
    )
    return both.reshape(-1, width)


def two_halves(capacity):
    rank = capacity.shape[1] // 2
    return jnp.concatenate([capacity[:, :rank], capacity[:, rank:]])


def solved_weights(own, other, side, capacity):
    upper, lower = jnp.where(side, own, other), jnp.where(side, other, own)
    rank = capacity.shape[1]
    return product_nt(upper, capacity[:rank]) + product_nt(lower, capacity[rank:])


def corrected(current, weights, solved, core):
    weights = ordered(weights, swapped(weights, CORE), core)
    return current - product_nt(weights, solved)


def per_device(
    right_sides,
    leaf_inverse,
    coupling_first,
    coupling_second,
    coupling_third,
    coupling_fourth,
    solved_first,
    solved_second,
    solved_third,
    solved_fourth,
    first_level_inverse,
    second_level_inverse,
    third_level_inverse,
    root_level_inverse,
):
    rank = coupling_first.shape[1]
    device_id = lax.axis_index("leaf")
    core, y_low, y_high, x_low, x_high = (
        (device_id >> place) & 1 == 1 for place in (0, 4, 5, 6, 7)
    )
    z = (device_id >> 1) & 7
    side_a, side_b, side_c = ((side >> z) & 1 == 1 for side in (SIDE_A, SIDE_B, SIDE_C))
    y_side = y_low != y_high
    sizes = [
        level.shape[0]
        for level in (second_level_inverse, third_level_inverse, root_level_inverse)
    ]
    orders = [
        jnp.asarray(tree_order(2**level, first_level_inverse.shape[0] >> level))
        for level in range(4)
    ]

    current = product_nt(right_sides, leaf_inverse)
    kept, away = halves(product_nn(current, coupling_first), core)

    near = two_halves(after(first_level_inverse, away))
    far = jnp.zeros((first_level_inverse.shape[0] - sum(sizes), 2 * rank), jnp.float32)
    far = [second_level_inverse, third_level_inverse, root_level_inverse, far]
    far = two_halves(after(jnp.concatenate(far), away))
    sums = kept + swapped(away, CORE)

    other, near_other, far_other = sent(Z_C, sums, near, far)
    cross_second, cross_third = after((solved_second, solved_third), sums)
    cross = by_rows(
        jnp.concatenate(
            [
                product_tn(cross_second, coupling_third),
                product_tn(cross_second, coupling_fourth),
                product_tn(cross_third, coupling_fourth),
            ]
        )
    )
    cross, cross_away = halves(cross, core, 3)
    cross_other = swapped(cross_away, CORE)
    sums = sums + other
    near, far = ordered(near, near_other, side_c, 2), ordered(far, far_other, side_c, 2)

    other, near_other, far_other = sent(Z_B, sums, near, far)
    cross, cross_away = halves(cross + after(cross_other, sums), y_side, 3)
    cross_other = swapped(cross_away, Y_A)
    sums = sums + other
    near, far = ordered(near, near_other, side_b, 2), ordered(far, far_other, side_b, 2)

    other, near_other = sent(Z_A, sums, near)
    cross = cross + after(cross_other, sums)
    last = cross.shape[0] // 3 * 2
    cross_other = swapped(cross[last:], Y_B)
    sums, near = sums + other, ordered(near, near_other, side_a, 2)

    other = swapped(sums, Y_A)
    near = ordered(near, swapped(near, CORE), core, 2)
    cross = jnp.concatenate([cross[:last], cross[last:] + after(cross_other, sums)])
    cross, cross_away = halves(cross, side_a, 3)
    cross_other = swapped(cross_away, Z_A)
    solved_first = product_nt(after(solved_first, sums), orders[0])
    first = solved_weights(sums, other, y_low, near)

    cross, cross_away = halves(cross + after(cross_other, first), side_b, 3)
    cross_other = swapped(cross_away, Z_B)
    far_other = swapped(after(far, first), Z_A)
    current = corrected(current, first, solved_first, core)

    sums = [
        product_nn(current, coupling)
        for coupling in (coupling_second, coupling_third, coupling_fourth)
    ]
    kept, away = halves(jnp.concatenate(sums), core, 3)
    share = kept.shape[0] // 3
    sums = kept + swapped(away, CORE)

    cross = cross + after(cross_other, away)
    other, cross_other = sent(Z_C, sums, cross)
    far = ordered(far, after(far_other, sums), side_a, 2).reshape(16, -1, rank)
    ends = [0, sizes[0], sizes[0] + sizes[1], sum(sizes)]
    far = [far[:, a:b].reshape(-1, rank) for a, b in zip(ends, ends[1:])]
    far_other = sent(Y_A, *far)
    solved_fourth = product_nt(after(solved_fourth, sums), orders[3])
    sums, cross = sums + other, cross + cross_other

    other, cross_other = sent(Z_B, sums, cross)
    far_other = after(far_other, sums)
    far = [ordered(own, got, y_low, 2) for own, got in zip(far, far_other)]
    far_other = sent(Y_B, *far[1:])
    capacity_other = swapped(far[0], CORE)
    sums, cross = sums + other, ordered(cross, cross_other, side_b, 3)

    other, cross_other = sent(Z_A, sums, cross)
    capacity = [ordered(far[0], after(capacity_other, sums), core, 2)]
    far_other = after(far_other, sums)
    far = [ordered(own, got, y_high, 2) for own, got in zip(far[1:], far_other)]
    far_other = swapped(far[1], X_A)
    capacity_other = swapped(far[0], CORE)
    sums, cross = sums + other, ordered(cross, cross_other, side_a, 3)

    other = swapped(sums, Y_A)
    cross_other = swapped(cross, Y_A)
    capacity.append(ordered(far[0], after(capacity_other, sums), core, 2))
    far = ordered(far[1], after(far_other, sums), x_low, 2)
    capacity_other = swapped(far, CORE)
    sums = sums + other

    own = sums[:share]
    other = swapped(own, Y_B)
    cross = ordered(cross, after(cross_other, sums), y_side, 3)
    cross_other = swapped(cross, CORE)
    capacity.append(ordered(far, after(capacity_other, sums), core, 2))
    second = product_nn(solved_weights(own, other, y_high, capacity[0]), orders[1])
    cross = ordered(cross, after(cross_other, other), core, 3)
    sums = sums[share:] - jnp.concatenate(
        [product_nn(second, cross[:rank]), product_nn(second, cross[rank : 2 * rank])]
    )

    other = swapped(sums, Y_B)
    second_other = swapped(after(second, sums), CORE)
    sums = sums + other

    own = sums[:share]
    other = swapped(own, X_A)
    second = ordered(second, after(second_other, sums), core)
    current = current - product_nt(second, solved_second)
    third = product_nn(solved_weights(own, other, x_low, capacity[1]), orders[2])
    sums = sums[share:] - product_nn(third, cross[2 * rank :])

    other = swapped(sums, X_A)
    third_other = swapped(after(third, sums), CORE)
    sums = sums + other

    other = swapped(sums, X_B)
    third = ordered(third, after(third_other, sums), core)
    current = after(current, sums) - product_nt(third, solved_third)
    fourth = solved_weights(sums, other, x_high, capacity[2])
    return corrected(current, fourth, solved_fourth, core)


def solution(mesh):
    in_specs = (P(None, "leaf"),) + (P("leaf", None),) * 13
    return jax.shard_map(
        per_device,
        mesh=mesh,
        in_specs=in_specs,
        out_specs=P(None, "leaf"),
        check_vma=False,
    )
```

```python
import jax
import jax.numpy as jnp
import numpy as np
from jax import lax
from jax.experimental.layout import Layout, with_layout_constraint
from jax.sharding import PartitionSpec as P

CORE, Y_A, Y_B, X_A, X_B, X_AB = (
    [i ^ mask for i in range(256)] for mask in (1, 16, 48, 64, 192, 128)
)


def ring_pairs(partner):
    return [i - i % 16 + 2 * partner[i // 2 % 8] + i % 2 for i in range(256)]


Z_A = ring_pairs([1, 0, 3, 2, 5, 4, 7, 6])
Z_B = ring_pairs([7, 2, 1, 4, 3, 6, 5, 0])
Z_C = ring_pairs([3, 6, 5, 0, 7, 2, 1, 4])
SIDE_A, SIDE_B, SIDE_C = 0b01100110, 0b10110100, 0b11101000
RING_ORDER = [0, 3, 4, 7, 1, 6, 2, 5]


def one_hot(source, size):
    matrix = np.zeros((len(source), size), np.float32)
    matrix[np.arange(len(source)), source] = 1
    return matrix


def ring_order(rows):
    source = [
        (z * 2 + core) * rows + row
        for core in range(2)
        for z in RING_ORDER
        for row in range(rows)
    ]
    return one_hot(source, len(source))


def tree_order(highs, pairs, rows):
    source = [
        (((high + pair) * 8 + z) * 2 + core) * rows + row
        for core in range(2)
        for high in highs
        for z in RING_ORDER
        for pair in pairs
        for _ in range(2)
        for row in range(rows)
    ]
    return one_hot(source, len(source) // 2)


def by_rows(value):
    return with_layout_constraint(value, Layout(major_to_minor=(0, 1)))


def after(value, token):
    return lax.optimization_barrier((value, token))[0]


def swapped(value, partner):
    return lax.ppermute(value, "leaf", list(enumerate(partner)))


def sent(partner, *parts):
    got = swapped(jnp.concatenate(parts), partner)
    ends = [0]
    for part in parts:
        ends.append(ends[-1] + part.shape[0])
    return [got[first:last] for first, last in zip(ends, ends[1:])]


def product(left, right, dims, precision=lax.Precision.HIGH):
    return lax.dot_general(
        left,
        right,
        ((dims[:1], dims[1:]), ((), ())),
        precision=precision,
        preferred_element_type=jnp.float32,
    )


def product_nn(left, right):
    return product(left, right, (1, 0))


def product_nt(left, right):
    return product(left, right, (1, 1))


def product_tn(left, right):
    return product(left, right, (0, 0))


def placed(part, offset, size):
    rest = size - offset - part.shape[0]
    return lax.pad(part, jnp.float32(0), ((offset, rest, 0), (0, 0, 0)))


def halves(value, side, blocks=1):
    value = value.reshape(blocks, 2, -1, value.shape[1])
    kept = jnp.where(side, value[:, 1], value[:, 0])
    other = jnp.where(side, value[:, 0], value[:, 1])
    return kept.reshape(-1, value.shape[3]), other.reshape(-1, value.shape[3])


def ordered(own, other, side, blocks=1):
    width = own.shape[1]
    own, other = own.reshape(blocks, -1, width), other.reshape(blocks, -1, width)
    both = jnp.where(
        side,
        jnp.concatenate([other, own], axis=1),
        jnp.concatenate([own, other], axis=1),
    )
    return both.reshape(-1, width)


def two_halves(*capacities):
    rank = capacities[0].shape[1] // 2
    return [part for one in capacities for part in (one[:, :rank], one[:, rank:])]


def solved_weights(own, other, side, capacity):
    upper, lower = jnp.where(side, own, other), jnp.where(side, other, own)
    rank = capacity.shape[1]
    return product_nt(upper, capacity[:rank]) + product_nt(lower, capacity[rank:])


def ordered_weights(own, other, side, capacity, order, rows):
    upper, lower = jnp.where(side, own, other), jnp.where(side, other, own)
    both = product_nt(jnp.concatenate([upper, lower]), capacity)
    both = both.reshape(2, -1, both.shape[1])
    first = np.arange(both.shape[2]) // rows % 2 == 0
    first = jnp.asarray(first[None].astype(np.float32))
    return product_nn(jnp.where(first == 1, both[0], both[1]), order)


def corrected(current, weights, solved, core):
    weights = ordered(weights, swapped(weights, CORE), core)
    return current - product_nt(weights, solved)


def per_device(
    right_sides,
    leaf_inverse,
    coupling_first,
    coupling_second,
    coupling_third,
    coupling_fourth,
    solved_first,
    solved_second,
    solved_third,
    solved_fourth,
    first_level_inverse,
    second_level_inverse,
    third_level_inverse,
    root_level_inverse,
):
    rank = coupling_first.shape[1]
    device_id = lax.axis_index("leaf")
    core, y_low, y_high, x_low, x_high = (
        (device_id >> place) & 1 == 1 for place in (0, 4, 5, 6, 7)
    )
    z = (device_id >> 1) & 7
    side_a, side_b, side_c = ((side >> z) & 1 == 1 for side in (SIDE_A, SIDE_B, SIDE_C))
    y_side = y_low != y_high
    rows = second_level_inverse.shape[0]
    orders = [
        ring_order(2 * rows),
        tree_order((0, 1), (0,), rows),
        tree_order((0, 1, 2, 3), (0,), rows // 2),
        tree_order((0, 2, 4, 6), (0, 1), rows // 4),
    ]
    orders = [jnp.asarray(order) for order in orders]

    sides = [core, y_low, y_high, x_low, x_high, y_side, side_a, side_b, side_c]
    sides, right_sides = lax.optimization_barrier((sides, right_sides))
    core, y_low, y_high, x_low, x_high, y_side, side_a, side_b, side_c = sides
    current = product_nt(right_sides, leaf_inverse)
    kept, away = halves(product_nn(current, coupling_first), core)

    near = jnp.concatenate(two_halves(after(first_level_inverse, away)))
    far = [second_level_inverse, third_level_inverse, root_level_inverse]
    far = two_halves(*after(far, away))
    size, offset, whole = 4 * rows, 0, 0
    for part in far[:4]:
        whole = whole + placed(part, offset, size)
        offset += part.shape[0]
    low = placed(far[4], offset, size) + placed(far[5], offset + rows // 4, size)
    offset += rows // 2
    high = placed(far[4], offset, size) + placed(far[5], offset + rows // 4, size)
    far = whole + jnp.where(y_low, high, low)
    near, far = lax.optimization_barrier((near, far))
    sums = kept + swapped(away, CORE)

    other, near_other, far_other = sent(Z_C, sums, near, far)
    cross_second, cross_third = after((solved_second, solved_third), sums)
    cross = by_rows(
        jnp.concatenate(
            [
                product_tn(cross_second, coupling_third),
                product_tn(cross_second, coupling_fourth),
                product_tn(cross_third, coupling_fourth),
            ]
        )
    )
    cross, cross_away = halves(cross, core, 3)
    cross_other = swapped(cross_away, CORE)
    sums = sums + other
    near, far = ordered(near, near_other, side_c, 2), ordered(far, far_other, side_c)

    sums, cross = lax.optimization_barrier((sums, cross + cross_other))
    other, near_other, far_other = sent(Z_B, sums, near, far)
    cross, cross_away = halves(cross, y_side, 3)
    cross_other = swapped(cross_away, Y_A)
    sums = sums + other
    near, far = ordered(near, near_other, side_b, 2), ordered(far, far_other, side_b)

    other, near_other = sent(Z_A, sums, near)
    cross, cross_away = halves(cross + after(cross_other, sums), side_a, 3)
    cross_other = swapped(cross_away, Z_A)
    sums, near = sums + other, ordered(near, near_other, side_a, 2)

    other = swapped(sums, Y_A)
    near = ordered(near, swapped(near, CORE), core, 2)
    cross, cross_away = halves(cross + after(cross_other, sums), side_b, 3)
    cross_other = swapped(cross_away, Z_B)
    solved_first = product_nt(after(solved_first, sums), orders[0])
    first = solved_weights(sums, other, y_low, near)

    far_other = swapped(after(far, first), Z_A)
    current = corrected(current, first, solved_first, core)

    sums = [
        product_nn(current, coupling)
        for coupling in (coupling_second, coupling_third, coupling_fourth)
    ]
    kept, away = halves(jnp.concatenate(sums), core, 3)
    share = kept.shape[0] // 3
    sums = kept + swapped(away, CORE)

    other = swapped(sums, Y_A)
    cross = cross + after(cross_other, away)
    cross_other = swapped(cross, Z_C)
    far = ordered(far, after(far_other, sums), side_a).reshape(8, -1, rank)
    ends = [0, 2 * rows, 3 * rows, 4 * rows]
    far = [far[:, a:b].reshape(-1, rank) for a, b in zip(ends, ends[1:])]
    sums = sums + other

    other = swapped(sums, Z_C)
    cross = cross + after(cross_other, sums)
    cross_other = swapped(cross, Y_A)
    far_other = sent(Y_A, *after(far, sums))
    sums, cross = sums + other, ordered(cross, after(cross_other, other), y_side, 3)

    other, cross_other = sent(Z_B, sums, cross)
    sums, cross = sums + other, ordered(cross, cross_other, side_b, 6)

    other, cross_other = sent(Z_A, sums, cross)
    far_other = after(far_other, sums)
    far[:2] = [ordered(own, got, y_low) for own, got in zip(far[:2], far_other)]
    far[2] = far[2] + far_other[2]
    far_other = sent(Y_B, *far[1:])
    capacity_other = swapped(far[0], CORE)
    sums, cross = sums + other, ordered(cross, cross_other, side_a, 6)
    capacity = [ordered(far[0], after(capacity_other, sums), core)]

    own = sums[:share]
    cross, last = cross[:rank], cross[rank:]
    other, last_other = sent(Y_B, own, last)
    cross_other = swapped(cross, CORE)
    far_other = after(far_other, sums)
    far = [ordered(own, got, y_high) for own, got in zip(far[1:], far_other)]
    far_other = swapped(far[1], X_A)
    capacity_other = swapped(far[0], CORE)
    second = ordered_weights(own, other, y_high, capacity[0], orders[1], rows)
    cross = ordered(cross, after(cross_other, other), core, 2)
    sums = sums[share:] - jnp.concatenate(
        [product_nn(second, cross[:rank]), product_nn(second, cross[rank:])]
    )

    other = swapped(sums, Y_B)
    second_other = swapped(after(second, sums), CORE)
    last = last + last_other
    last_other = swapped(last, CORE)
    capacity.append(ordered(far[0], after(capacity_other, sums), core))
    far = ordered(far[1], after(far_other, sums), x_low)
    capacity_other = swapped(far, CORE)
    sums = sums + other

    own = sums[:share]
    other = swapped(own, X_A)
    second = ordered(second, after(second_other, sums), core)
    current = current - product_nt(second, solved_second)
    third = ordered_weights(own, other, x_low, capacity[1], orders[2], rows // 2)
    last = ordered(last, after(last_other, sums), core)
    sums = sums[share:] - product_nn(third, last)

    other = swapped(sums, X_A)
    sibling = swapped(sums, X_B) + swapped(sums, X_AB)
    capacity.append(ordered(far, after(capacity_other, third), core))
    third_other = swapped(after(third, sums), CORE)
    sums = sums + other
    third = ordered(third, after(third_other, sums), core)
    current = after(current, sums) - product_nt(third, solved_third)
    fourth = ordered_weights(sums, sibling, x_high, capacity[2], orders[3], rows // 4)
    return corrected(current, fourth, solved_fourth, core)


def solution(mesh):
    in_specs = (P(None, "leaf"),) + (P("leaf", None),) * 13
    return jax.shard_map(
        per_device,
        mesh=mesh,
        in_specs=in_specs,
        out_specs=P(None, "leaf"),
        check_vma=False,
    )
```

```python
import jax
import jax.numpy as jnp
import numpy as np
from jax import lax
from jax.experimental.layout import Layout, with_layout_constraint
from jax.sharding import PartitionSpec as P

CORE, Y_A, Y_B, X_A, X_B, X_AB = (
    [i ^ mask for i in range(256)] for mask in (1, 16, 48, 64, 192, 128)
)


def ring_pairs(partner):
    return [i - i % 16 + 2 * partner[i // 2 % 8] + i % 2 for i in range(256)]


Z_A = ring_pairs([1, 0, 3, 2, 5, 4, 7, 6])
Z_B = ring_pairs([7, 2, 1, 4, 3, 6, 5, 0])
Z_C = ring_pairs([3, 6, 5, 0, 7, 2, 1, 4])
SIDE_A, SIDE_B, SIDE_C = 0b01100110, 0b10110100, 0b11101000
RING_ORDER = [0, 3, 4, 7, 1, 6, 2, 5]


def one_hot(source, size):
    matrix = np.zeros((len(source), size), np.float32)
    matrix[np.arange(len(source)), source] = 1
    return matrix


def ring_order(rows):
    source = [
        (z * 2 + core) * rows + row
        for core in range(2)
        for z in RING_ORDER
        for row in range(rows)
    ]
    return one_hot(source, len(source))


def tree_order(highs, pairs, rows):
    source = [
        (((high + pair) * 8 + z) * 2 + core) * rows + row
        for core in range(2)
        for high in highs
        for z in RING_ORDER
        for pair in pairs
        for _ in range(2)
        for row in range(rows)
    ]
    return one_hot(source, len(source) // 2)


def by_rows(value):
    return with_layout_constraint(value, Layout(major_to_minor=(0, 1)))


def after(value, token):
    return lax.optimization_barrier((value, token))[0]


def swapped(value, partner):
    return lax.ppermute(value, "leaf", list(enumerate(partner)))


def sent(partner, *parts):
    got = swapped(jnp.concatenate(parts), partner)
    ends = [0]
    for part in parts:
        ends.append(ends[-1] + part.shape[0])
    return [got[first:last] for first, last in zip(ends, ends[1:])]


def product(left, right, dims, precision=lax.Precision.HIGH):
    return lax.dot_general(
        left,
        right,
        ((dims[:1], dims[1:]), ((), ())),
        precision=precision,
        preferred_element_type=jnp.float32,
    )


def product_nn(left, right):
    return product(left, right, (1, 0))


def product_nt(left, right):
    return product(left, right, (1, 1))


def product_tn(left, right):
    return product(left, right, (0, 0))


def placed(part, offset, size):
    rest = size - offset - part.shape[0]
    return lax.pad(part, jnp.float32(0), ((offset, rest, 0), (0, 0, 0)))


def halves(value, side, blocks=1):
    value = value.reshape(blocks, 2, -1, value.shape[1])
    kept = jnp.where(side, value[:, 1], value[:, 0])
    other = jnp.where(side, value[:, 0], value[:, 1])
    return kept.reshape(-1, value.shape[3]), other.reshape(-1, value.shape[3])


def ordered(own, other, side, blocks=1):
    width = own.shape[1]
    own, other = own.reshape(blocks, -1, width), other.reshape(blocks, -1, width)
    both = jnp.where(
        side,
        jnp.concatenate([other, own], axis=1),
        jnp.concatenate([own, other], axis=1),
    )
    return both.reshape(-1, width)


def two_halves(*capacities):
    rank = capacities[0].shape[1] // 2
    return [part for one in capacities for part in (one[:, :rank], one[:, rank:])]


def solved_weights(own, other, side, capacity):
    upper, lower = jnp.where(side, own, other), jnp.where(side, other, own)
    rank = capacity.shape[1]
    return product_nt(upper, capacity[:rank]) + product_nt(lower, capacity[rank:])


def ordered_weights(own, other, side, capacity, order, rows):
    upper, lower = jnp.where(side, own, other), jnp.where(side, other, own)
    both = product_nt(jnp.concatenate([upper, lower]), capacity)
    both = both.reshape(2, -1, both.shape[1])
    first = np.arange(both.shape[2]) // rows % 2 == 0
    first = jnp.asarray(first[None].astype(np.float32))
    return product_nn(jnp.where(first == 1, both[0], both[1]), order)


def corrected(current, weights, solved, core):
    weights = ordered(weights, swapped(weights, CORE), core)
    return current - product_nt(weights, solved)


def per_device(
    right_sides,
    leaf_inverse,
    coupling_first,
    coupling_second,
    coupling_third,
    coupling_fourth,
    solved_first,
    solved_second,
    solved_third,
    solved_fourth,
    first_level_inverse,
    second_level_inverse,
    third_level_inverse,
    root_level_inverse,
):
    rank = coupling_first.shape[1]
    device_id = lax.axis_index("leaf")
    core, y_low, y_high, x_low, x_high = (
        (device_id >> place) & 1 == 1 for place in (0, 4, 5, 6, 7)
    )
    z = (device_id >> 1) & 7
    side_a, side_b, side_c = ((side >> z) & 1 == 1 for side in (SIDE_A, SIDE_B, SIDE_C))
    y_side = y_low != y_high
    rows = second_level_inverse.shape[0]
    orders = [
        ring_order(2 * rows),
        tree_order((0, 1), (0,), rows),
        tree_order((0, 1, 2, 3), (0,), rows // 2),
        tree_order((0, 2, 4, 6), (0, 1), rows // 4),
    ]
    orders = [jnp.asarray(order) for order in orders]

    sides = [core, y_low, y_high, x_low, x_high, y_side, side_a, side_b, side_c]
    sides, right_sides = lax.optimization_barrier((sides, right_sides))
    core, y_low, y_high, x_low, x_high, y_side, side_a, side_b, side_c = sides
    current = product_nt(right_sides, leaf_inverse)
    kept, away = halves(product_nn(current, coupling_first), core)

    near = jnp.concatenate(two_halves(after(first_level_inverse, away)))
    far = [second_level_inverse, third_level_inverse, root_level_inverse]
    far = two_halves(*after(far, away))
    size, offset, whole = 4 * rows, 0, 0
    for part in far[:4]:
        whole = whole + placed(part, offset, size)
        offset += part.shape[0]
    low = placed(far[4], offset, size) + placed(far[5], offset + rows // 4, size)
    offset += rows // 2
    high = placed(far[4], offset, size) + placed(far[5], offset + rows // 4, size)
    far = whole + jnp.where(y_low, high, low)
    near, far = lax.optimization_barrier((near, far))
    sums = kept + swapped(away, CORE)

    other, near_other, far_other = sent(Z_C, sums, near, far)
    cross_second, cross_third = after((solved_second, solved_third), sums)
    cross = by_rows(
        jnp.concatenate(
            [
                product_tn(cross_second, coupling_third),
                product_tn(cross_second, coupling_fourth),
                product_tn(cross_third, coupling_fourth),
            ]
        )
    )
    cross, cross_away = halves(cross, core, 3)
    cross_other = swapped(cross_away, CORE)
    sums = sums + other
    near, far = ordered(near, near_other, side_c, 2), ordered(far, far_other, side_c)

    sums, cross = lax.optimization_barrier((sums, cross + cross_other))
    other, near_other, far_other = sent(Z_B, sums, near, far)
    cross, cross_away = halves(cross, y_side, 3)
    cross_other = swapped(cross_away, Y_A)
    sums = sums + other
    near, far = ordered(near, near_other, side_b, 2), ordered(far, far_other, side_b)

    other, near_other = sent(Z_A, sums, near)
    cross, cross_away = halves(cross + after(cross_other, sums), side_a, 3)
    cross_other = swapped(cross_away, Z_A)
    sums, near = sums + other, ordered(near, near_other, side_a, 2)

    other = swapped(sums, Y_A)
    near = ordered(near, swapped(near, CORE), core, 2)
    cross, cross_away = halves(cross + after(cross_other, sums), side_b, 3)
    cross_other = swapped(cross_away, Z_B)
    solved_first = product_nt(after(solved_first, sums), orders[0])
    first = solved_weights(sums, other, y_low, near)

    far_other = swapped(after(far, first), Z_A)
    current = corrected(current, first, solved_first, core)

    sums = [
        product_nn(current, coupling)
        for coupling in (coupling_second, coupling_third, coupling_fourth)
    ]
    kept, away = halves(jnp.concatenate(sums), core, 3)
    share = kept.shape[0] // 3
    sums = kept + swapped(away, CORE)

    other = swapped(sums, Y_A)
    cross = cross + after(cross_other, away)
    cross_other = swapped(cross, Z_C)
    sums = sums + other
    far = ordered(far, after(far_other, sums), side_a).reshape(8, -1, rank)
    ends = [0, 2 * rows, 3 * rows, 4 * rows]
    far = [far[:, a:b].reshape(-1, rank) for a, b in zip(ends, ends[1:])]

    other = swapped(sums, Z_C)
    cross = cross + after(cross_other, sums)
    cross_other = swapped(cross, Y_A)
    far_other = sent(Y_A, *far)
    sums, cross = sums + other, ordered(cross, after(cross_other, other), y_side, 3)

    other, cross_other = sent(Z_B, sums, cross)
    sums, cross = sums + other, ordered(cross, cross_other, side_b, 6)

    other, cross_other = sent(Z_A, sums, cross)
    far_other = after(far_other, sums)
    far[:2] = [ordered(own, got, y_low) for own, got in zip(far[:2], far_other)]
    far[2] = far[2] + far_other[2]
    far_other = sent(Y_B, *far[1:])
    capacity_other = swapped(far[0], CORE)
    sums, cross = sums + other, ordered(cross, cross_other, side_a, 6)
    capacity = [ordered(far[0], after(capacity_other, sums), core)]

    own = sums[:share]
    cross, last = cross[:rank], cross[rank:]
    other, last_other = sent(Y_B, own, last)
    cross_other = swapped(cross, CORE)
    second = ordered_weights(own, other, y_high, capacity[0], orders[1], rows)
    cross = ordered(cross, after(cross_other, other), core, 2)
    sums = sums[share:] - jnp.concatenate(
        [product_nn(second, cross[:rank]), product_nn(second, cross[rank:])]
    )

    other = swapped(sums, Y_B)
    far_other = after(far_other, sums)
    far = [ordered(own, got, y_high) for own, got in zip(far[1:], far_other)]
    far_other = swapped(far[1], X_A)
    capacity_other = swapped(far[0], CORE)
    second_other = swapped(after(second, sums), CORE)
    last = last + last_other
    last_other = swapped(last, CORE)
    capacity.append(ordered(far[0], after(capacity_other, sums), core))
    far = ordered(far[1], after(far_other, sums), x_low)
    capacity_other = swapped(far, CORE)
    sums = sums + other

    own = sums[:share]
    other = swapped(own, X_A)
    second = ordered(second, after(second_other, sums), core)
    current = current - product_nt(second, solved_second)
    third = ordered_weights(own, other, x_low, capacity[1], orders[2], rows // 2)
    last = ordered(last, after(last_other, sums), core)
    sums = sums[share:] - product_nn(third, last)

    other = swapped(sums, X_A)
    sibling = swapped(sums, X_B) + swapped(sums, X_AB)
    capacity.append(ordered(far, after(capacity_other, third), core))
    third_other = swapped(after(third, sums), CORE)
    sums = sums + other
    third = ordered(third, after(third_other, sums), core)
    current = after(current, sums) - product_nt(third, solved_third)
    fourth = ordered_weights(sums, sibling, x_high, capacity[2], orders[3], rows // 4)
    return corrected(current, fourth, solved_fourth, core)


def solution(mesh):
    in_specs = (P(None, "leaf"),) + (P("leaf", None),) * 13
    return jax.shard_map(
        per_device,
        mesh=mesh,
        in_specs=in_specs,
        out_specs=P(None, "leaf"),
        check_vma=False,
    )
```

```python
import jax
import jax.numpy as jnp
import numpy as np
from jax import lax
from jax.experimental.layout import Layout, with_layout_constraint
from jax.sharding import PartitionSpec as P

CORE, Y_A, Y_B, X_A, X_B, X_AB = (
    [i ^ mask for i in range(256)] for mask in (1, 16, 48, 64, 192, 128)
)


def ring_pairs(partner):
    return [i - i % 16 + 2 * partner[i // 2 % 8] + i % 2 for i in range(256)]


Z_A = ring_pairs([1, 0, 3, 2, 5, 4, 7, 6])
Z_B = ring_pairs([7, 2, 1, 4, 3, 6, 5, 0])
Z_C = ring_pairs([3, 6, 5, 0, 7, 2, 1, 4])
SIDE_A, SIDE_B, SIDE_C = 0b01100110, 0b10110100, 0b11101000
RING_ORDER = [0, 3, 4, 7, 1, 6, 2, 5]


def one_hot(source, size):
    matrix = np.zeros((len(source), size), np.float32)
    matrix[np.arange(len(source)), source] = 1
    return matrix


def ring_order(rows):
    source = [
        (z * 2 + core) * rows + row
        for core in range(2)
        for z in RING_ORDER
        for row in range(rows)
    ]
    return one_hot(source, len(source))


def tree_order(highs, pairs, rows):
    source = [
        (((high + pair) * 8 + z) * 2 + core) * rows + row
        for core in range(2)
        for high in highs
        for z in RING_ORDER
        for pair in pairs
        for _ in range(2)
        for row in range(rows)
    ]
    return one_hot(source, len(source) // 2)


def by_rows(value):
    return with_layout_constraint(value, Layout(major_to_minor=(0, 1)))


def after(value, token):
    return lax.optimization_barrier((value, token))[0]


def swapped(value, partner):
    return lax.ppermute(value, "leaf", list(enumerate(partner)))


def sent(partner, *parts):
    got = swapped(jnp.concatenate(parts), partner)
    ends = [0]
    for part in parts:
        ends.append(ends[-1] + part.shape[0])
    return [got[first:last] for first, last in zip(ends, ends[1:])]


def product(left, right, dims, precision=lax.Precision.HIGH):
    return lax.dot_general(
        left,
        right,
        ((dims[:1], dims[1:]), ((), ())),
        precision=precision,
        preferred_element_type=jnp.float32,
    )


def product_nn(left, right):
    return product(left, right, (1, 0))


def product_nt(left, right):
    return product(left, right, (1, 1))


def product_tn(left, right):
    return product(left, right, (0, 0))


def placed(part, offset, size):
    rest = size - offset - part.shape[0]
    return lax.pad(part, jnp.float32(0), ((offset, rest, 0), (0, 0, 0)))


def halves(value, side, blocks=1):
    value = value.reshape(blocks, 2, -1, value.shape[1])
    kept = jnp.where(side, value[:, 1], value[:, 0])
    other = jnp.where(side, value[:, 0], value[:, 1])
    return kept.reshape(-1, value.shape[3]), other.reshape(-1, value.shape[3])


def ordered(own, other, side, blocks=1):
    width = own.shape[1]
    own, other = own.reshape(blocks, -1, width), other.reshape(blocks, -1, width)
    both = jnp.where(
        side,
        jnp.concatenate([other, own], axis=1),
        jnp.concatenate([own, other], axis=1),
    )
    return both.reshape(-1, width)


def two_halves(*capacities):
    rank = capacities[0].shape[1] // 2
    return [part for one in capacities for part in (one[:, :rank], one[:, rank:])]


def solved_weights(own, other, side, capacity):
    upper, lower = jnp.where(side, own, other), jnp.where(side, other, own)
    rank = capacity.shape[1]
    return product_nt(upper, capacity[:rank]) + product_nt(lower, capacity[rank:])


def in_tree_order(capacity, order, rows):
    first = (np.arange(capacity.shape[0]) // rows % 2 == 0)[:, None]
    parts = [product_tn(jnp.asarray(order * half), capacity) for half in (first, ~first)]
    return jnp.concatenate(parts, axis=1)


def ordered_weights(own, other, side, capacity):
    upper, lower = jnp.where(side, own, other), jnp.where(side, other, own)
    return product_nt(jnp.concatenate([upper, lower], axis=1), capacity)


def corrected(current, weights, solved, core):
    weights = ordered(weights, swapped(weights, CORE), core)
    return current - product_nt(weights, solved)


def per_device(
    right_sides,
    leaf_inverse,
    coupling_first,
    coupling_second,
    coupling_third,
    coupling_fourth,
    solved_first,
    solved_second,
    solved_third,
    solved_fourth,
    first_level_inverse,
    second_level_inverse,
    third_level_inverse,
    root_level_inverse,
):
    rank = coupling_first.shape[1]
    device_id = lax.axis_index("leaf")
    core, y_low, y_high, x_low, x_high = (
        (device_id >> place) & 1 == 1 for place in (0, 4, 5, 6, 7)
    )
    z = (device_id >> 1) & 7
    side_a, side_b, side_c = ((side >> z) & 1 == 1 for side in (SIDE_A, SIDE_B, SIDE_C))
    y_side = y_low != y_high
    rows = second_level_inverse.shape[0]
    orders = [
        ring_order(2 * rows),
        tree_order((0, 1), (0,), rows),
        tree_order((0, 1, 2, 3), (0,), rows // 2),
        tree_order((0, 2, 4, 6), (0, 1), rows // 4),
    ]

    sides = [core, y_low, y_high, x_low, x_high, y_side, side_a, side_b, side_c]
    sides, right_sides = lax.optimization_barrier((sides, right_sides))
    core, y_low, y_high, x_low, x_high, y_side, side_a, side_b, side_c = sides
    current = product_nt(right_sides, leaf_inverse)
    kept, away = halves(product_nn(current, coupling_first), core)

    near = jnp.concatenate(two_halves(after(first_level_inverse, away)))
    far = [second_level_inverse, third_level_inverse, root_level_inverse]
    far = two_halves(*after(far, away))
    size, offset, whole = 4 * rows, 0, 0
    for part in far[:4]:
        whole = whole + placed(part, offset, size)
        offset += part.shape[0]
    low = placed(far[4], offset, size) + placed(far[5], offset + rows // 4, size)
    offset += rows // 2
    high = placed(far[4], offset, size) + placed(far[5], offset + rows // 4, size)
    far = whole + jnp.where(y_low, high, low)
    near, far = lax.optimization_barrier((near, far))
    sums = kept + swapped(away, CORE)

    other, near_other, far_other = sent(Z_C, sums, near, far)
    cross_second, cross_third = after((solved_second, solved_third), sums)
    cross = by_rows(
        jnp.concatenate(
            [
                product_tn(cross_second, coupling_third),
                product_tn(cross_second, coupling_fourth),
                product_tn(cross_third, coupling_fourth),
            ]
        )
    )
    cross, cross_away = halves(cross, core, 3)
    cross_other = swapped(cross_away, CORE)
    sums = sums + other
    near, far = ordered(near, near_other, side_c, 2), ordered(far, far_other, side_c)

    sums, cross = lax.optimization_barrier((sums, cross + cross_other))
    other, near_other, far_other = sent(Z_B, sums, near, far)
    cross, cross_away = halves(cross, y_side, 3)
    cross_other = swapped(cross_away, Y_A)
    sums = sums + other
    near, far = ordered(near, near_other, side_b, 2), ordered(far, far_other, side_b)

    other, near_other = sent(Z_A, sums, near)
    cross, cross_away = halves(cross + after(cross_other, sums), side_a, 3)
    cross_other = swapped(cross_away, Z_A)
    sums, near = sums + other, ordered(near, near_other, side_a, 2)

    other = swapped(sums, Y_A)
    near = ordered(near, swapped(near, CORE), core, 2)
    cross, cross_away = halves(cross + after(cross_other, sums), side_b, 3)
    cross_other = swapped(cross_away, Z_B)
    solved_first = product_nt(after(solved_first, sums), jnp.asarray(orders[0]))
    first = solved_weights(sums, other, y_low, near)

    far_other = swapped(after(far, first), Z_A)
    current = corrected(current, first, solved_first, core)

    sums = [
        product_nn(current, coupling)
        for coupling in (coupling_second, coupling_third, coupling_fourth)
    ]
    kept, away = halves(jnp.concatenate(sums), core, 3)
    share = kept.shape[0] // 3
    sums = kept + swapped(away, CORE)

    other = swapped(sums, Y_A)
    cross = cross + after(cross_other, away)
    cross_other = swapped(cross, Z_C)
    sums = sums + other
    far = ordered(far, after(far_other, sums), side_a).reshape(8, -1, rank)
    ends = [0, 2 * rows, 3 * rows, 4 * rows]
    far = [far[:, a:b].reshape(-1, rank) for a, b in zip(ends, ends[1:])]

    other = swapped(sums, Z_C)
    cross = cross + after(cross_other, sums)
    cross_other = swapped(cross, Y_A)
    far_other = sent(Y_A, *far)
    sums, cross = sums + other, ordered(cross, after(cross_other, other), y_side, 3)

    other, cross_other = sent(Z_B, sums, cross)
    sums, cross = sums + other, ordered(cross, cross_other, side_b, 6)

    other, cross_other = sent(Z_A, sums, cross)
    far_other = after(far_other, sums)
    far[:2] = [ordered(own, got, y_low) for own, got in zip(far[:2], far_other)]
    far[2] = far[2] + far_other[2]
    far_other = sent(Y_B, *far[1:])
    capacity_other = swapped(far[0], CORE)
    sums, cross = sums + other, ordered(cross, cross_other, side_a, 6)
    capacity = [ordered(far[0], after(capacity_other, sums), core)]
    capacity[0] = in_tree_order(capacity[0], orders[1], rows)

    own = sums[:share]
    cross, last = cross[:rank], cross[rank:]
    other, last_other = sent(Y_B, own, last)
    cross_other = swapped(cross, CORE)
    second = ordered_weights(own, other, y_high, capacity[0])
    cross = ordered(cross, after(cross_other, other), core, 2)
    sums = sums[share:] - jnp.concatenate(
        [product_nn(second, cross[:rank]), product_nn(second, cross[rank:])]
    )

    other = swapped(sums, Y_B)
    far_other = after(far_other, sums)
    far = [ordered(own, got, y_high) for own, got in zip(far[1:], far_other)]
    far_other = swapped(far[1], X_A)
    capacity_other = swapped(far[0], CORE)
    second_other = swapped(after(second, sums), CORE)
    last = last + last_other
    last_other = swapped(last, CORE)
    capacity.append(ordered(far[0], after(capacity_other, sums), core))
    capacity[1] = in_tree_order(capacity[1], orders[2], rows // 2)
    far = ordered(far[1], after(far_other, sums), x_low)
    capacity_other = swapped(far, CORE)
    sums = sums + other

    own = sums[:share]
    other = swapped(own, X_A)
    second = ordered(second, after(second_other, sums), core)
    current = current - product_nt(second, solved_second)
    third = ordered_weights(own, other, x_low, capacity[1])
    last = ordered(last, after(last_other, sums), core)
    sums = sums[share:] - product_nn(third, last)

    other = swapped(sums, X_A)
    sibling = swapped(sums, X_B) + swapped(sums, X_AB)
    capacity.append(ordered(far, after(capacity_other, third), core))
    capacity[2] = in_tree_order(capacity[2], orders[3], rows // 4)
    third_other = swapped(after(third, sums), CORE)
    sums = sums + other
    third = ordered(third, after(third_other, sums), core)
    current = after(current, sums) - product_nt(third, solved_third)
    fourth = ordered_weights(sums, sibling, x_high, capacity[2])
    return corrected(current, fourth, solved_fourth, core)


def solution(mesh):
    in_specs = (P(None, "leaf"),) + (P("leaf", None),) * 13
    return jax.shard_map(
        per_device,
        mesh=mesh,
        in_specs=in_specs,
        out_specs=P(None, "leaf"),
        check_vma=False,
    )
```
